32 devices in a mesh: dp: 4 (over y, core), expert: 8 (over z, x).
Axes of the slice: x: 2, y: 2, z: 4, core: 2. Of those that a mesh axis runs over, the one named last changes fastest.
Arguments:
- tokens: bfloat16 [4096, 2048], P(('dp', 'expert')), may hold values from -6 to 6
- tangents: bfloat16 [4096, 2048], P(('dp', 'expert')), may hold values from -6 to 6
- cotangents: bfloat16 [4096, 2048], P(('dp', 'expert')), may hold values from -6 to 6
- routes: int32 [4096, 2], P(('dp', 'expert')), may hold values from 0 to 7, all different within a row; in each aligned block of 128 rows (0 to 127, 128 to 255, ...) at most 64 rows name the same one
- gates: bfloat16 [4096, 2], P(('dp', 'expert')), may hold values from 0.19921875 to 1
- w_up: bfloat16 [8, 2048, 768], P('expert'), may hold values from -0.125 to 0.125
- w_down: bfloat16 [8, 768, 2048], P('expert'), may hold values from -0.21875 to 0.21875
- v_up: bfloat16 [8, 2048, 768], P('expert'), may hold values from -0.125 to 0.125
Outputs:
- hvp_tokens: bfloat16 [4096, 2048], P(('dp', 'expert'))
- hvp_up: bfloat16 [8, 2048, 768], P('expert', 'dp')
- hvp_down: bfloat16 [8, 768, 2048], P('expert', None, 'dp')
The draws below stay inside these ranges and needn't reach their ends.
Inputs may be any that keep to these rules, and one draw needn't show every extreme that they name: `routes`: A token's 2 experts differ. Among the 128 tokens of one device no expert is named more than 64 times, and in every draw some device names some expert exactly 64 times.
All inputs are finite; a program needn't handle non-finite values.
Results may differ from the reference program's by a relative error of at most 0.014.
Values may be sent and summed in bfloat16 or wider, within the bound.
A program may use at most 128 MiB of HBM per device.

```python
import math
import jax
import jax.numpy as jnp
import numpy as np
from jax import lax

D = 2048
FF = 768
TOK_DEV = 128
TOP = 2
EXPERTS = 8
CAP = 64
TOKENS = 4096
N_DP = 4
N_EXPERT = 8


def block_scale(stream_key, extent, pieces, low, largest):
    factor_of, own = 1.0, jax.random.fold_in(stream_key, 6)
    for position, parts in pieces:
        draws = jnp.exp(jax.random.uniform(jax.random.fold_in(own, position), (parts,), jnp.float32, low / len(pieces), largest / len(pieces)))
        factor_of = factor_of * jnp.repeat(draws, extent[position] // parts).reshape([-1 if axis == position else 1 for axis in range(len(extent))])
    return factor_of


def assign_block(key, own, number, rows, amount, top, most, skew):
    ranking = jax.random.permutation(key, amount)
    packed, ordinary = portions_of(amount, rows * top, most, skew, True), portions_of(amount, rows * top, most, skew, False)
    places = jnp.arange(amount)

    def named(lengths, offset_by):
        used = int((lengths > 0).sum())
        fixed = max(1, used // 4)
        shifted = fixed + (places - fixed + offset_by * (used - fixed)) % max(1, amount - fixed)
        return jnp.zeros((amount,), jnp.int32).at[ranking[jnp.where(places < fixed, places, shifted)]].set(jnp.asarray(lengths, jnp.int32))

    lengths = jnp.where(number % 4 == 0, named(packed, number // 4), named(ordinary, number - number // 4 - 1))
    mixed = jax.random.permutation(jax.random.fold_in(own, 3), amount)
    donor, receiver = mixed[0:amount // 2 * 2:2], mixed[1:amount // 2 * 2:2]
    margin = jnp.minimum(lengths[donor] - 1, most - lengths[receiver]) // 2
    margin = jnp.where((donor == ranking[0]) | (receiver == ranking[0]) | (lengths[receiver] == 0), 0, jnp.maximum(margin, 0))
    shifted = jax.random.randint(jax.random.fold_in(own, 4), (amount // 2,), 0, 1 << 20) % (margin + 1)
    lengths = lengths.at[donor].add(-shifted).at[receiver].add(shifted)
    labels = jnp.searchsorted(jnp.cumsum(lengths), jnp.arange(rows * top), side="right").astype(jnp.int32)
    table = labels.reshape(top, rows).T
    table = table[jax.random.permutation(jax.random.fold_in(own, 1), rows)]
    offset_by = jax.random.randint(jax.random.fold_in(own, 2), (rows, 1), 0, top)
    return jnp.take_along_axis(table, (jnp.arange(top)[None, :] + offset_by) % top, axis=1)


def portions_of(amount, total, reach, skew, full):
    loads = [(1 << 20) // math.isqrt(standing ** skew) + 1 for standing in range(1, amount + 1)]
    largest = reach if full else min(reach, max(-(-total // amount), total * loads[0] // sum(loads)))
    least = 1 if total - largest >= amount - 1 else 0
    given, rest = [largest] + [least] * (amount - 1), total - largest - least * (amount - 1)
    while rest > 0:
        free = [i for i in range(1, amount) if given[i] < largest] or [i for i in range(1, amount) if given[i] < reach]
        whole, budget = sum([loads[i] for i in free]), rest
        for i in free:
            addition = min(reach - given[i], max(1, budget * loads[i] // whole), rest)
            given[i] = given[i] + addition
            rest = rest - addition
    return np.array(given)


def scatter_about(key, dims, width, most, split=(), held_as=jnp.bfloat16):
    values = jax.random.normal(key, dims, jnp.float32) * width
    if len(split) > 0:
        values = block_scale(key, dims, split, -0.22, 0.18) * values
    return jnp.clip(values, min=-most, max=most).astype(held_as)


def setup_inputs(seed: int = 0) -> dict:
    streams_of = jax.random.split(jax.random.key(seed), 9)
    tokens = scatter_about(streams_of[0], (TOKENS, D), 1.0, 6.0, ((0, 32),))
    tangents = scatter_about(streams_of[1], (TOKENS, D), 1.0, 6.0, ((0, 32),))
    cotangents = scatter_about(streams_of[2], (TOKENS, D), 1.0, 6.0, ((0, 32),))
    routes_keys = jax.random.split(jax.random.fold_in(streams_of[3], 1), TOKENS // TOK_DEV)
    routes_turns = jax.random.permutation(jax.random.fold_in(streams_of[3], 3), TOKENS // TOK_DEV)
    routes = jax.vmap(lambda own, number: assign_block(jax.random.fold_in(streams_of[3], 2), own, number, TOK_DEV, EXPERTS, TOP, CAP, 2))(routes_keys, routes_turns).reshape((TOKENS, TOP))
    gates = jnp.clip(0.19921875 + 0.80078125 * jax.random.uniform(streams_of[4], (TOKENS, TOP), jnp.float32) ** block_scale(streams_of[4], (TOKENS, TOP), ((0, 32),), -0.2, 0.2), 0.19921875, 1.0).astype(jnp.bfloat16)
    w_up = scatter_about(streams_of[5], (EXPERTS, D, FF), D ** -0.5, 0.125, ((0, 8),))
    w_down = scatter_about(streams_of[6], (EXPERTS, FF, D), FF ** -0.5, 0.21875, ((0, 8),))
    v_up = scatter_about(streams_of[7], (EXPERTS, D, FF), D ** -0.5, 0.125, ((0, 8),))
    return dict(tokens=tokens, tangents=tangents, cotangents=cotangents, routes=routes, gates=gates, w_up=w_up, w_down=w_down, v_up=v_up)


def slot_table(route_ids, expert_count, capacity):
    token_count, route_count = route_ids.shape
    flat_ids = route_ids.reshape(token_count * route_count)
    onehot = (flat_ids[:, None] == jnp.arange(expert_count, dtype=jnp.int32)[None, :]).astype(jnp.int32)
    before = jnp.cumsum(onehot, axis=0) - onehot
    slot_rank = lax.optimization_barrier(jnp.sum(before * onehot, axis=1))
    target = flat_ids * capacity + slot_rank
    slot_owner = jnp.full((expert_count * capacity,), -1, jnp.int32).at[target].set(jnp.arange(token_count * route_count, dtype=jnp.int32))
    return (target, slot_owner)

def gather_slots(rows, slot_owner, route_count):
    valid = slot_owner >= 0
    safe = jnp.where(valid, slot_owner, 0) // route_count
    picked = jnp.take(rows, safe, axis=0)
    return jnp.where(valid[:, None], picked, jnp.zeros_like(picked))

def gather_gates(gate_rows, slot_owner):
    valid = slot_owner >= 0
    flat_gate = gate_rows.reshape(-1)
    picked = jnp.take(flat_gate, jnp.where(valid, slot_owner, 0), axis=0)
    return jnp.where(valid, picked, jnp.zeros_like(picked))

def expert_terms(primal, tangent, cotan, gate_slot, up_proj, down_proj, dir_up):
    pre_act = jnp.dot(primal, up_proj, preferred_element_type=jnp.float32)
    pre_tan = jnp.dot(tangent, up_proj, preferred_element_type=jnp.float32) + jnp.dot(primal, dir_up, preferred_element_type=jnp.float32)
    sigmoid_z = jax.nn.sigmoid(pre_act)
    first_der = sigmoid_z * (1.0 + pre_act * (1.0 - sigmoid_z))
    second_der = sigmoid_z * (1.0 - sigmoid_z) * (2.0 + pre_act * (1.0 - 2.0 * sigmoid_z))
    hidden_tan = (first_der * pre_tan).astype(jnp.bfloat16)
    scaled_cot = (gate_slot.astype(jnp.float32)[:, None] * cotan.astype(jnp.float32)).astype(jnp.bfloat16)
    back_hid = jnp.dot(scaled_cot, down_proj.T, preferred_element_type=jnp.float32)
    back_pre = (back_hid * first_der).astype(jnp.bfloat16)
    back_tan = (back_hid * second_der * pre_tan).astype(jnp.bfloat16)
    input_hvp = (jnp.dot(back_tan, up_proj.T, preferred_element_type=jnp.float32) + jnp.dot(back_pre, dir_up.T, preferred_element_type=jnp.float32)).astype(jnp.bfloat16)
    hvp_first = jnp.dot(tangent.T, back_pre, preferred_element_type=jnp.float32) + jnp.dot(primal.T, back_tan, preferred_element_type=jnp.float32)
    hvp_second = jnp.dot(scaled_cot.T, hidden_tan, preferred_element_type=jnp.float32)
    return (input_hvp, hvp_first, hvp_second)

def reference(tokens, tangents, cotangents, routes, gates, w_up, w_down, v_up):
    blocks = N_DP * N_EXPERT
    tok_blocks = tokens.reshape(blocks, TOK_DEV, D)
    tan_blocks = tangents.reshape(blocks, TOK_DEV, D)
    cot_blocks = cotangents.reshape(blocks, TOK_DEV, D)
    route_blocks = routes.reshape(blocks, TOK_DEV, TOP)
    gate_blocks = gates.reshape(blocks, TOK_DEV * TOP)
    targets, owners = jax.vmap(lambda r: slot_table(r, EXPERTS, CAP))(route_blocks)
    scale = 1.0 / math.sqrt(TOK_DEV * TOP * N_DP)
    block_ids = jnp.arange(blocks, dtype=jnp.int32)[:, None]

    def one_expert(carry, expert_id):
        own = lax.dynamic_slice_in_dim(owners, expert_id * CAP, CAP, 1)
        gather_all = jax.vmap(lambda rows, o: gather_slots(rows, o, TOP))
        primal = gather_all(tok_blocks, own).reshape(N_DP, N_EXPERT * CAP, D)
        tangent = gather_all(tan_blocks, own).reshape(N_DP, N_EXPERT * CAP, D)
        cotan = gather_all(cot_blocks, own).reshape(N_DP, N_EXPERT * CAP, D)
        gate_slot = jax.vmap(gather_gates)(gate_blocks, own).reshape(N_DP, N_EXPERT * CAP)
        up_proj = w_up[expert_id]
        down_proj = w_down[expert_id]
        dir_up = v_up[expert_id]
        input_hvp, hvp_first, hvp_second = lax.map(lambda a: expert_terms(a[0], a[1], a[2], a[3], up_proj, down_proj, dir_up), (primal, tangent, cotan, gate_slot))
        first_parts = lax.optimization_barrier((hvp_first * scale).astype(jnp.bfloat16))
        second_parts = lax.optimization_barrier((hvp_second * scale).astype(jnp.bfloat16))
        sum_first = lax.optimization_barrier(jnp.sum(first_parts.astype(jnp.float32), axis=0)).astype(jnp.bfloat16)
        sum_second = lax.optimization_barrier(jnp.sum(second_parts.astype(jnp.float32), axis=0)).T.astype(jnp.bfloat16)
        valid = own >= 0
        token_ids = jnp.where(valid, own, 0) // TOP
        rows_back = input_hvp.reshape(blocks, CAP, D).astype(jnp.float32)
        rows_back = jnp.where(valid[:, :, None], rows_back, jnp.zeros_like(rows_back))
        carry = carry.at[jnp.broadcast_to(block_ids, token_ids.shape), token_ids].add(rows_back)
        return (carry, (sum_first, sum_second))
    start = jnp.zeros((blocks, TOK_DEV, D), jnp.float32)
    total, (hvp_up, hvp_down) = lax.scan(one_expert, start, jnp.arange(EXPERTS, dtype=jnp.int32))
    hvp_tokens = total.reshape(TOKENS, D).astype(jnp.bfloat16)
    return (hvp_tokens, hvp_up, hvp_down)
```

```python
import functools
import math

import jax
import jax.numpy as jnp
from jax import lax
from jax.experimental import pallas as pl
from jax.experimental.pallas import tpu as pltpu
from jax.sharding import PartitionSpec as P

MESH = pl.DeviceIdType.MESH
F32 = jnp.float32
BF16 = jnp.bfloat16


def route_rows(routes, gates, expert_count):
    token_count = routes.shape[0]
    hit = routes[:, :, None] == jnp.arange(expert_count, dtype=jnp.int32)[None, None, :]
    mask = jnp.any(hit, axis=1)
    rank = jnp.cumsum(mask.astype(jnp.int32), axis=0) - 1
    slot = jnp.where(mask, rank, -1).astype(F32)
    gate = jnp.sum(jnp.where(hit, gates.astype(F32)[:, :, None], 0.0), axis=1)
    return jnp.concatenate([slot.T, gate.T], axis=0).reshape(2 * expert_count, token_count)


def layer_kernel(
    n, inner, cap,
    meta, tok, tan, cot, w_up, w_down, v_up,
    out, rows, hid,
    mbuf, gbuf, sbuf, hback, hsend, pbuf, psend, wu, wd, vu,
    load_sem, own_send, fwd_send, g_recv, x_send, x_recv, h_send, h_recv, p_send, p_recv,
):
    me = lax.axis_index("expert")
    z = me // inner
    x = me % inner
    experts = n * inner
    tokens = gbuf.shape[2]

    def at(outer_pos, inner_pos):
        return {"expert": outer_pos * inner + inner_pos}

    def peer(o):
        return lax.rem(x + o, inner)

    own = [
        pltpu.make_async_copy(src, dst, load_sem.at[i])
        for i, (src, dst) in enumerate(
            [
                (meta, mbuf.at[z]),
                (tok, gbuf.at[0, z]),
                (tan, gbuf.at[1, z]),
                (cot, gbuf.at[2, z]),
                (w_up, wu),
                (v_up, vu),
                (w_down, wd),
            ]
        )
    ]
    for c in own:
        c.start()

    barrier = pltpu.get_barrier_semaphore()
    has_left = z > 0
    has_right = z < n - 1
    for cond, pos in ((has_left, z - 1), (has_right, z + 1)):

        @pl.when(cond)
        def _():
            pl.semaphore_signal(barrier, inc=1, device_id=at(pos, x), device_id_type=MESH)

    for o in range(1, inner):
        pl.semaphore_signal(barrier, inc=1, device_id=at(z, peer(o)), device_id_type=MESH)
    for o in range(1, n):
        far = lax.rem(z + o, n)

        @pl.when(jnp.logical_and(far != z - 1, far != z + 1))
        def _():
            pl.semaphore_signal(barrier, inc=1, device_id=at(far, x), device_id_type=MESH)

    pl.semaphore_wait(barrier, n - 1 + inner - 1)

    def block(a, j):
        return mbuf.at[j] if a == 0 else gbuf.at[a - 1, j]

    def hop(a, j, pos, send_sem):
        return pltpu.make_async_remote_copy(
            src_ref=block(a, j),
            dst_ref=block(a, j),
            send_sem=send_sem,
            recv_sem=g_recv.at[a, j],
            device_id=at(pos, x),
            device_id_type=MESH,
        )

    for a in range(4):
        own[a].wait()

        @pl.when(has_left)
        def _():
            hop(a, z, z - 1, own_send.at[a, 0]).start()

        @pl.when(has_right)
        def _():
            hop(a, z, z + 1, own_send.at[a, 1]).start()

    near = jnp.minimum(z, n - 1 - z)
    left_half = z < n - 1 - z

    def source(k):
        d = (k + 1) // 2
        toward = jnp.where(left_half, d, -d)
        close = jnp.where(k % 2 == 1, z + toward, z - toward)
        return jnp.where(k <= 2 * near, close, jnp.where(left_half, k, n - 1 - k))

    def picks(j):
        slots = lax.broadcasted_iota(jnp.int32, (cap, tokens), 0).astype(F32)
        ones, gated = [], []
        for o in range(inner):
            e = z * inner + peer(o)
            hit = mbuf[j, pl.ds(e, 1), :] == slots
            ones.append(jnp.where(hit, 1.0, 0.0))
            gated.append(jnp.where(hit, mbuf[j, pl.ds(experts + e, 1), :], 0.0))
        return jnp.concatenate(ones, axis=0), jnp.concatenate(gated, axis=0)

    def x_copy(a, j, o):
        return pltpu.make_async_remote_copy(
            src_ref=sbuf.at[j, a, o - 1],
            dst_ref=rows.at[j, a, pl.ds((inner - o) * cap, cap)],
            send_sem=x_send.at[a, j, o - 1],
            recv_sem=x_recv.at[a, j, inner - o - 1],
            device_id=at(z, peer(o)),
            device_id_type=MESH,
        )

    def x_arrival(a, j, o):
        return pltpu.make_async_remote_copy(
            src_ref=sbuf.at[j, a, o - 1],
            dst_ref=rows.at[j, a, pl.ds(o * cap, cap)],
            send_sem=x_send.at[a, j, o - 1],
            recv_sem=x_recv.at[a, j, o - 1],
            device_id=at(z, peer(o)),
            device_id_type=MESH,
        )

    def h_copy(j, o):
        return pltpu.make_async_remote_copy(
            src_ref=hsend.at[j, o - 1],
            dst_ref=hback.at[j, pl.ds((inner - o) * cap, cap)],
            send_sem=h_send.at[j, o - 1],
            recv_sem=h_recv.at[j, inner - o - 1],
            device_id=at(z, peer(o)),
            device_id_type=MESH,
        )

    def h_arrival(j, o):
        return pltpu.make_async_remote_copy(
            src_ref=hsend.at[j, o - 1],
            dst_ref=hback.at[j, pl.ds(o * cap, cap)],
            send_sem=h_send.at[j, o - 1],
            recv_sem=h_recv.at[j, o - 1],
            device_id=at(z, peer(o)),
            device_id_type=MESH,
        )

    def p_copy(j):
        return pltpu.make_async_remote_copy(
            src_ref=psend.at[j],
            dst_ref=pbuf.at[z],
            send_sem=p_send.at[j],
            recv_sem=p_recv.at[z],
            device_id=at(j, x),
            device_id_type=MESH,
        )

    def p_arrival(j):
        return pltpu.make_async_remote_copy(
            src_ref=psend.at[j],
            dst_ref=pbuf.at[j],
            send_sem=p_send.at[j],
            recv_sem=p_recv.at[j],
            device_id=at(j, x),
            device_id_type=MESH,
        )

    def bring(k):
        j = source(k)
        forward_left = jnp.logical_and(j > z, has_left)
        forward_right = jnp.logical_and(j < z, has_right)

        def take(a):
            @pl.when(j != z)
            def _():
                hop(a, j, z, fwd_send.at[a, j]).wait_recv()

                @pl.when(forward_left)
                def _():
                    hop(a, j, z - 1, fwd_send.at[a, j]).start()

                @pl.when(forward_right)
                def _():
                    hop(a, j, z + 1, fwd_send.at[a, j]).start()

        take(0)
        ones, gated = picks(j)
        for a in range(3):
            take(a + 1)
            pick = (gated if a == 2 else ones).astype(BF16)
            got = jnp.dot(pick, gbuf[a, j], preferred_element_type=F32).astype(BF16)
            rows[j, a, pl.ds(0, cap)] = got[:cap]
            for o in range(1, inner):
                sbuf[j, a, o - 1] = got[o * cap : (o + 1) * cap]
                x_copy(a, j, o).start()

    def nt(a, b):
        return lax.dot_general(a, b, (((1,), (1,)), ((), ())), preferred_element_type=F32)

    def work(k):
        j = source(k)
        for a in range(3):
            for o in range(1, inner):
                x_arrival(a, j, o).wait_recv()
        count = inner * cap
        both = rows[j, pl.ds(0, 2)].reshape(2 * count, rows.shape[3])
        up = jnp.dot(both, wu[...], preferred_element_type=F32)
        act = up[:count]
        act_tan = up[count:] + jnp.dot(rows[j, 0], vu[...], preferred_element_type=F32)
        s = 1.0 / (1.0 + jnp.exp(-act))
        s1 = s * (1.0 + act * (1.0 - s))
        s2 = s * (1.0 - s) * (2.0 + act * (1.0 - 2.0 * s))
        back = nt(rows[j, 2], wd[...])
        gz = (back * s1).astype(BF16)
        gzd = (back * s2 * act_tan).astype(BF16)
        hid[0, j] = (s1 * act_tan).astype(BF16)
        hid[1, j] = gz
        hid[2, j] = gzd
        ha = (nt(gzd, wu[...]) + nt(gz, vu[...])).astype(BF16)
        hback[j, pl.ds(0, cap)] = ha[:cap]
        for o in range(1, inner):
            hsend[j, o - 1] = ha[o * cap : (o + 1) * cap]
            h_copy(j, o).start()

    def give(k):
        j = source(k)
        for o in range(1, inner):
            h_arrival(j, o).wait_recv()
        ones, _ = picks(j)
        part = jnp.dot(ones.T.astype(BF16), hback[j], preferred_element_type=F32).astype(BF16)

        @pl.when(j == z)
        def _():
            pbuf[z] = part

        @pl.when(j != z)
        def _():
            psend[j] = part
            p_copy(j).start()

    def step(k, carry):
        @pl.when(k < n)
        def _():
            bring(k)

        @pl.when(k == 1)
        def _():
            for c in own[4:]:
                c.wait()

        @pl.when(jnp.logical_and(k >= 1, k < n + 1))
        def _():
            work(k - 1)

        @pl.when(k >= 2)
        def _():
            give(k - 2)

        return carry

    lax.fori_loop(0, n + 2, step, 0)

    for j in range(n):

        @pl.when(j != z)
        def _():
            p_arrival(j).wait_recv()

    total = pbuf[0].astype(F32)
    for j in range(1, n):
        total = total + pbuf[j].astype(F32)
    out[...] = total.astype(BF16)

    for a in range(4):

        @pl.when(has_left)
        def _():
            hop(a, z, z, own_send.at[a, 0]).wait_send()

        @pl.when(has_right)
        def _():
            hop(a, z, z, own_send.at[a, 1]).wait_send()

    for j in range(n):
        forwarded = jnp.logical_or(
            jnp.logical_and(j > z, has_left), jnp.logical_and(j < z, has_right)
        )

        @pl.when(forwarded)
        def _():
            for a in range(4):
                hop(a, j, z, fwd_send.at[a, j]).wait_send()

        for o in range(1, inner):
            for a in range(3):
                x_copy(a, j, o).wait_send()
            h_copy(j, o).wait_send()

        @pl.when(j != z)
        def _():
            p_copy(j).wait_send()


def per_device(tokens, tangents, cotangents, routes, gates, w_up, w_down, v_up):
    token_count, width = tokens.shape
    route_count = routes.shape[1]
    experts = lax.axis_size("expert")
    replicas = lax.axis_size("dp")
    hidden = w_up.shape[2]
    cap = max(2, token_count * route_count * 2 // experts)
    scale = 1.0 / math.sqrt(token_count * route_count * replicas)
    n = 4
    inner = experts // n
    meta = route_rows(routes, gates, experts)
    count = inner * cap
    vmem = pl.BlockSpec(memory_space=pltpu.VMEM)
    hbm = pl.BlockSpec(memory_space=pl.ANY)
    dma = pltpu.SemaphoreType.DMA
    hvp_tokens, rows, hid = pl.pallas_call(
        functools.partial(layer_kernel, n, inner, cap),
        out_shape=(
            jax.ShapeDtypeStruct((token_count, width), BF16),
            jax.ShapeDtypeStruct((n, 3, count, width), BF16),
            jax.ShapeDtypeStruct((3, n, count, hidden), BF16),
        ),
        in_specs=[hbm] * 7,
        out_specs=(vmem, vmem, vmem),
        scratch_shapes=[
            pltpu.VMEM((n, 2 * experts, token_count), F32),
            pltpu.VMEM((3, n, token_count, width), BF16),
            pltpu.VMEM((n, 3, inner - 1, cap, width), BF16),
            pltpu.VMEM((n, count, width), BF16),
            pltpu.VMEM((n, inner - 1, cap, width), BF16),
            pltpu.VMEM((n, token_count, width), BF16),
            pltpu.VMEM((n, token_count, width), BF16),
            pltpu.VMEM((width, hidden), BF16),
            pltpu.VMEM((hidden, width), BF16),
            pltpu.VMEM((width, hidden), BF16),
            dma((7,)),
            dma((4, 2)),
            dma((4, n)),
            dma((4, n)),
            dma((3, n, inner - 1)),
            dma((3, n, inner - 1)),
            dma((n, inner - 1)),
            dma((n, inner - 1)),
            dma((n,)),
            dma((n,)),
        ],
        compiler_params=pltpu.CompilerParams(
            collective_id=0, has_side_effects=True, vmem_limit_bytes=58 * 1024 * 1024
        ),
        cost_estimate=pl.CostEstimate(
            flops=12 * n * count * width * hidden, bytes_accessed=20_000_000, transcendentals=0
        ),
    )(meta, tokens, tangents, cotangents, w_up[0], w_down[0], v_up[0])

    def tn(a, b):
        return lax.dot_general(a, b, (((0,), (0,)), ((), ())), preferred_element_type=F32)

    primal, tangent, cotan = (rows[:, a].reshape(n * count, width) for a in range(3))
    hd, gz, gzd = (hid[a].reshape(n * count, hidden) for a in range(3))
    first = tn(tangent, gz) + tn(primal, gzd)
    second = tn(cotan, hd)
    summed = lax.psum_scatter(
        (jnp.concatenate([first, second], axis=1) * scale).astype(BF16),
        "dp",
        scatter_dimension=0,
        tiled=True,
    ).astype(F32)
    hvp_up = summed[:, :hidden].astype(BF16)[None]
    hvp_down = summed[:, hidden:].T.astype(BF16)[None]
    return (hvp_tokens, hvp_up, hvp_down)


def solution(mesh):
    in_specs = (P(("dp", "expert"), None),) * 5 + (P("expert", None, None),) * 3
    out_specs = (P(("dp", "expert"), None), P("expert", "dp", None), P("expert", None, "dp"))
    return jax.shard_map(
        per_device, mesh=mesh, in_specs=in_specs, out_specs=out_specs, check_vma=False
    )
```

```python
import functools
import math

import jax
import jax.numpy as jnp
from jax import lax
from jax.experimental import pallas as pl
from jax.experimental.pallas import tpu as pltpu
from jax.sharding import PartitionSpec as P

MESH = pl.DeviceIdType.MESH
F32 = jnp.float32
BF16 = jnp.bfloat16


def route_rows(routes, gates, expert_count):
    token_count = routes.shape[0]
    hit = routes[:, :, None] == jnp.arange(expert_count, dtype=jnp.int32)[None, None, :]
    mask = jnp.any(hit, axis=1)
    rank = jnp.cumsum(mask.astype(jnp.int32), axis=0) - 1
    slot = jnp.where(mask, rank, -1).astype(F32)
    gate = jnp.sum(jnp.where(hit, gates.astype(F32)[:, :, None], 0.0), axis=1)
    return jnp.concatenate([slot.T, gate.T], axis=0).reshape(2 * expert_count, token_count)


def layer_kernel(
    n, inner, cap, planes, scale,
    meta, tok, tan, cot, w_up, w_down, v_up,
    out, out_up, out_down,
    rows, hid, mbuf, gbuf, sbuf, hback, pbuf, wu, wd, vu,
    acc_up, acc_down, core_out_up, core_out_down, core_in_up, core_in_down,
    plane_out_up, plane_out_down, plane_in_up, plane_in_down,
    load_sem, own_send, fwd_send, g_recv, x_send, x_recv, h_send, h_recv, p_send, p_recv,
    core_send, core_recv, plane_send, plane_recv,
):
    me = lax.axis_index("expert")
    z = me // inner
    x = me % inner
    experts = n * inner
    tokens = gbuf.shape[2]
    rep = lax.axis_index("dp")
    y = rep // 2
    core = rep % 2
    part = acc_up.shape[1]

    def at(outer_pos, inner_pos):
        return {"expert": outer_pos * inner + inner_pos}

    def peer(o):
        return lax.rem(x + o, inner)

    def plane(o):
        return lax.rem(y + o, planes)

    own = [
        pltpu.make_async_copy(src, dst, load_sem.at[i])
        for i, (src, dst) in enumerate(
            [
                (meta, mbuf.at[z]),
                (tok, gbuf.at[0, z]),
                (tan, gbuf.at[1, z]),
                (cot, gbuf.at[2, z]),
                (w_up, wu),
                (v_up, vu),
                (w_down, wd),
            ]
        )
    ]
    for c in own:
        c.start()

    barrier = pltpu.get_barrier_semaphore()
    has_left = z > 0
    has_right = z < n - 1
    for cond, pos in ((has_left, z - 1), (has_right, z + 1)):

        @pl.when(cond)
        def _():
            pl.semaphore_signal(barrier, inc=1, device_id=at(pos, x), device_id_type=MESH)

    for o in range(1, inner):
        pl.semaphore_signal(barrier, inc=1, device_id=at(z, peer(o)), device_id_type=MESH)
    for o in range(1, n):
        far = lax.rem(z + o, n)

        @pl.when(jnp.logical_and(far != z - 1, far != z + 1))
        def _():
            pl.semaphore_signal(barrier, inc=1, device_id=at(far, x), device_id_type=MESH)

    pl.semaphore_signal(
        barrier, inc=1, device_id={"dp": y * 2 + 1 - core}, device_id_type=MESH
    )
    for o in range(1, planes):
        pl.semaphore_signal(
            barrier, inc=1, device_id={"dp": plane(o) * 2 + core}, device_id_type=MESH
        )

    pl.semaphore_wait(barrier, n - 1 + inner - 1 + planes)

    def block(a, j):
        return mbuf.at[j] if a == 0 else gbuf.at[a - 1, j]

    def hop(a, j, pos, send_sem):
        return pltpu.make_async_remote_copy(
            src_ref=block(a, j),
            dst_ref=block(a, j),
            send_sem=send_sem,
            recv_sem=g_recv.at[a, j],
            device_id=at(pos, x),
            device_id_type=MESH,
        )

    for a in range(4):
        own[a].wait()

        @pl.when(has_left)
        def _():
            hop(a, z, z - 1, own_send.at[a, 0]).start()

        @pl.when(has_right)
        def _():
            hop(a, z, z + 1, own_send.at[a, 1]).start()

    acc_up[...] = jnp.zeros_like(acc_up)
    acc_down[...] = jnp.zeros_like(acc_down)

    near = jnp.minimum(z, n - 1 - z)
    left_half = z < n - 1 - z

    def source(k):
        d = (k + 1) // 2
        toward = jnp.where(left_half, d, -d)
        close = jnp.where(k % 2 == 1, z + toward, z - toward)
        return jnp.where(k <= 2 * near, close, jnp.where(left_half, k, n - 1 - k))

    def picks(j):
        slots = lax.broadcasted_iota(jnp.int32, (cap, tokens), 0).astype(F32)
        ones, gated = [], []
        for o in range(inner):
            e = z * inner + peer(o)
            hit = mbuf[j, pl.ds(e, 1), :] == slots
            ones.append(jnp.where(hit, 1.0, 0.0))
            gated.append(jnp.where(hit, mbuf[j, pl.ds(experts + e, 1), :], 0.0))
        return jnp.concatenate(ones, axis=0), jnp.concatenate(gated, axis=0)

    def x_copy(a, j, o):
        return pltpu.make_async_remote_copy(
            src_ref=sbuf.at[j, a, o - 1],
            dst_ref=rows.at[j, a, pl.ds((inner - o) * cap, cap)],
            send_sem=x_send.at[a, j, o - 1],
            recv_sem=x_recv.at[a, j, inner - o - 1],
            device_id=at(z, peer(o)),
            device_id_type=MESH,
        )

    def x_arrival(a, j, o):
        return pltpu.make_async_remote_copy(
            src_ref=sbuf.at[j, a, o - 1],
            dst_ref=rows.at[j, a, pl.ds(o * cap, cap)],
            send_sem=x_send.at[a, j, o - 1],
            recv_sem=x_recv.at[a, j, o - 1],
            device_id=at(z, peer(o)),
            device_id_type=MESH,
        )

    def h_copy(j, o):
        return pltpu.make_async_remote_copy(
            src_ref=sbuf.at[j, 0, o - 1],
            dst_ref=hback.at[j, pl.ds((inner - o) * cap, cap)],
            send_sem=h_send.at[j, o - 1],
            recv_sem=h_recv.at[j, inner - o - 1],
            device_id=at(z, peer(o)),
            device_id_type=MESH,
        )

    def h_arrival(j, o):
        return pltpu.make_async_remote_copy(
            src_ref=sbuf.at[j, 0, o - 1],
            dst_ref=hback.at[j, pl.ds(o * cap, cap)],
            send_sem=h_send.at[j, o - 1],
            recv_sem=h_recv.at[j, o - 1],
            device_id=at(z, peer(o)),
            device_id_type=MESH,
        )

    def p_copy(j):
        return pltpu.make_async_remote_copy(
            src_ref=gbuf.at[0, j],
            dst_ref=pbuf.at[lax.rem(z - j + n, n) - 1],
            send_sem=p_send.at[j],
            recv_sem=p_recv.at[lax.rem(z - j + n, n) - 1],
            device_id=at(j, x),
            device_id_type=MESH,
        )

    def p_arrival(o):
        return pltpu.make_async_remote_copy(
            src_ref=gbuf.at[0, lax.rem(z + o, n)],
            dst_ref=pbuf.at[o - 1],
            send_sem=p_send.at[lax.rem(z + o, n)],
            recv_sem=p_recv.at[o - 1],
            device_id=at(lax.rem(z + o, n), x),
            device_id_type=MESH,
        )

    def bring(k):
        j = source(k)
        forward_left = jnp.logical_and(j > z, has_left)
        forward_right = jnp.logical_and(j < z, has_right)

        def take(a):
            @pl.when(j != z)
            def _():
                hop(a, j, z, fwd_send.at[a, j]).wait_recv()

                @pl.when(forward_left)
                def _():
                    hop(a, j, z - 1, fwd_send.at[a, j]).start()

                @pl.when(forward_right)
                def _():
                    hop(a, j, z + 1, fwd_send.at[a, j]).start()

        take(0)
        ones, gated = picks(j)
        for a in range(3):
            take(a + 1)
            pick = (gated if a == 2 else ones).astype(BF16)
            got = jnp.dot(pick, gbuf[a, j], preferred_element_type=F32).astype(BF16)
            rows[j, a, pl.ds(0, cap)] = got[:cap]
            for o in range(1, inner):
                sbuf[j, a, o - 1] = got[o * cap : (o + 1) * cap]
                x_copy(a, j, o).start()

    def nt(a, b):
        return lax.dot_general(a, b, (((1,), (1,)), ((), ())), preferred_element_type=F32)

    def tn(a, b):
        return lax.dot_general(a, b, (((0,), (0,)), ((), ())), preferred_element_type=F32)

    def part_up(j, c):
        columns = pl.ds(pl.multiple_of(c * part, part), part)
        left = rows[j, pl.ds(0, 2), :, columns].reshape(2 * inner * cap, part)
        return tn(left, hid[j, pl.ds(0, 2)].reshape(2 * inner * cap, hid.shape[3]))

    def part_down(j, c):
        columns = pl.ds(pl.multiple_of(c * part, part), part)
        return tn(hid[j, 2], rows[j, 2, :, columns])

    def gather_part(j, c, carry):
        acc_up[c] += part_up(j, c)
        acc_down[c] += part_down(j, c)
        return carry

    core_out, core_in = (core_out_up, core_out_down), (core_in_up, core_in_down)
    plane_out, plane_in = (plane_out_up, plane_out_down), (plane_in_up, plane_in_down)
    accs, parts = (acc_up, acc_down), (part_up, part_down)

    def core_copy(half, yy):
        return pltpu.make_async_remote_copy(
            src_ref=core_out[half].at[yy],
            dst_ref=core_in[half].at[yy],
            send_sem=core_send.at[half, yy],
            recv_sem=core_recv.at[half, yy],
            device_id={"dp": y * 2 + 1 - core},
            device_id_type=MESH,
        )

    def plane_copy(half, o):
        return pltpu.make_async_remote_copy(
            src_ref=plane_out[half].at[o - 1],
            dst_ref=plane_in[half].at[planes - o - 1],
            send_sem=plane_send.at[half, o - 1],
            recv_sem=plane_recv.at[half, planes - o - 1],
            device_id={"dp": plane(o) * 2 + core},
            device_id_type=MESH,
        )

    def plane_arrival(half, o):
        return pltpu.make_async_remote_copy(
            src_ref=plane_out[half].at[o - 1],
            dst_ref=plane_in[half].at[o - 1],
            send_sem=plane_send.at[half, o - 1],
            recv_sem=plane_recv.at[half, o - 1],
            device_id={"dp": plane(o) * 2 + core},
            device_id_type=MESH,
        )

    def share(j):
        for o in range(1, planes + 1):
            yy = plane(o)
            for half in range(2):
                c = yy * 2 + 1 - core
                mine = accs[half][c] + parts[half](j, c)
                core_out[half][yy] = (mine * scale).astype(BF16)
                core_copy(half, yy).start()
            for half in range(2):
                c = yy * 2 + core
                mine = (accs[half][c] + parts[half](j, c)) * scale
                if o < planes:
                    core_copy(half, yy).wait_recv()
                    mine = mine + core_in[half][yy].astype(F32)
                    plane_out[half][o - 1] = mine.astype(BF16)
                    plane_copy(half, o).start()
                else:
                    accs[half][c] = mine

    def work(k):
        j = source(k)
        for a in range(3):
            for o in range(1, inner):
                x_arrival(a, j, o).wait_recv()
        count = inner * cap
        both = rows[j, pl.ds(0, 2)].reshape(2 * count, rows.shape[3])
        up = jnp.dot(both, wu[...], preferred_element_type=F32)
        act = up[:count]
        act_tan = up[count:] + jnp.dot(rows[j, 0], vu[...], preferred_element_type=F32)
        s = 1.0 / (1.0 + jnp.exp(-act))
        s1 = s * (1.0 + act * (1.0 - s))
        s2 = s * (1.0 - s) * (2.0 + act * (1.0 - 2.0 * s))
        back = nt(rows[j, 2], wd[...])
        gz = (back * s1).astype(BF16)
        gzd = (back * s2 * act_tan).astype(BF16)
        hid[j, 0] = gzd
        hid[j, 1] = gz
        hid[j, 2] = (s1 * act_tan).astype(BF16)

        @pl.when(k == n - 1)
        def _():
            share(j)

        ha = (nt(gzd, wu[...]) + nt(gz, vu[...])).astype(BF16)
        hback[j, pl.ds(0, cap)] = ha[:cap]
        for o in range(1, inner):
            x_copy(0, j, o).wait_send()
            sbuf[j, 0, o - 1] = ha[o * cap : (o + 1) * cap]
            h_copy(j, o).start()

        @pl.when(k < n - 1)
        def _():
            lax.fori_loop(0, 2 * planes, functools.partial(gather_part, j), 0)

    def sent(a, j):
        @pl.when(jnp.logical_and(j == z, has_left))
        def _():
            hop(a, z, z, own_send.at[a, 0]).wait_send()

        @pl.when(jnp.logical_and(j == z, has_right))
        def _():
            hop(a, z, z, own_send.at[a, 1]).wait_send()

        forwarded = jnp.logical_or(
            jnp.logical_and(j > z, has_left), jnp.logical_and(j < z, has_right)
        )

        @pl.when(forwarded)
        def _():
            hop(a, j, z, fwd_send.at[a, j]).wait_send()

    def give(k):
        j = source(k)
        for o in range(1, inner):
            h_arrival(j, o).wait_recv()
        ones, _ = picks(j)
        part = jnp.dot(ones.T.astype(BF16), hback[j], preferred_element_type=F32).astype(BF16)

        sent(1, j)
        gbuf[0, j] = part

        @pl.when(j != z)
        def _():
            p_copy(j).start()

    def step(k, carry):
        @pl.when(k < n)
        def _():
            bring(k)

        @pl.when(k == 1)
        def _():
            for c in own[4:]:
                c.wait()

        @pl.when(jnp.logical_and(k >= 1, k < n + 1))
        def _():
            work(k - 1)

        @pl.when(k >= 2)
        def _():
            give(k - 2)

        return carry

    lax.fori_loop(0, n + 2, step, 0)

    total = gbuf[0, z].astype(F32)
    for o in range(1, n):
        p_arrival(o).wait_recv()
        total = total + pbuf[o - 1].astype(F32)
    out[...] = total.astype(BF16)

    for half, result in enumerate((out_up, out_down)):
        core_copy(half, y).wait_recv()
        total = accs[half][y * 2 + core] + core_in[half][y].astype(F32)
        for o in range(1, planes):
            plane_arrival(half, o).wait_recv()
            total = total + plane_in[half][o - 1].astype(F32)
        result[...] = total.astype(BF16)
        for o in range(1, planes):
            plane_copy(half, o).wait_send()
        for yy in range(planes):
            core_copy(half, yy).wait_send()

    for j in range(n):
        for a in (0, 2, 3):
            sent(a, j)

        for o in range(1, inner):
            for a in range(1, 3):
                x_copy(a, j, o).wait_send()
            h_copy(j, o).wait_send()

        @pl.when(j != z)
        def _():
            p_copy(j).wait_send()


def per_device(tokens, tangents, cotangents, routes, gates, w_up, w_down, v_up):
    token_count, width = tokens.shape
    route_count = routes.shape[1]
    experts = lax.axis_size("expert")
    replicas = lax.axis_size("dp")
    hidden = w_up.shape[2]
    cap = max(2, token_count * route_count * 2 // experts)
    scale = 1.0 / math.sqrt(token_count * route_count * replicas)
    n = 4
    inner = experts // n
    meta = route_rows(routes, gates, experts)
    count = inner * cap
    planes = replicas // 2
    part = width // replicas
    vmem = pl.BlockSpec(memory_space=pltpu.VMEM)
    hbm = pl.BlockSpec(memory_space=pl.ANY)
    dma = pltpu.SemaphoreType.DMA
    up, down = (part, hidden), (hidden, part)
    hvp_tokens, hvp_up, hvp_down = pl.pallas_call(
        functools.partial(layer_kernel, n, inner, cap, planes, scale),
        out_shape=(
            jax.ShapeDtypeStruct((token_count, width), BF16),
            jax.ShapeDtypeStruct(up, BF16),
            jax.ShapeDtypeStruct(down, BF16),
        ),
        in_specs=[hbm] * 7,
        out_specs=(vmem, vmem, vmem),
        scratch_shapes=[
            pltpu.VMEM((n, 3, count, width), BF16),
            pltpu.VMEM((n, 3, count, hidden), BF16),
            pltpu.VMEM((n, 2 * experts, token_count), F32),
            pltpu.VMEM((3, n, token_count, width), BF16),
            pltpu.VMEM((n, 3, inner - 1, cap, width), BF16),
            pltpu.VMEM((n, count, width), BF16),
            pltpu.VMEM((n - 1, token_count, width), BF16),
            pltpu.VMEM((width, hidden), BF16),
            pltpu.VMEM((hidden, width), BF16),
            pltpu.VMEM((width, hidden), BF16),
            pltpu.VMEM((replicas,) + up, F32),
            pltpu.VMEM((replicas,) + down, F32),
            pltpu.VMEM((planes,) + up, BF16),
            pltpu.VMEM((planes,) + down, BF16),
            pltpu.VMEM((planes,) + up, BF16),
            pltpu.VMEM((planes,) + down, BF16),
            pltpu.VMEM((planes - 1,) + up, BF16),
            pltpu.VMEM((planes - 1,) + down, BF16),
            pltpu.VMEM((planes - 1,) + up, BF16),
            pltpu.VMEM((planes - 1,) + down, BF16),
            dma((7,)),
            dma((4, 2)),
            dma((4, n)),
            dma((4, n)),
            dma((3, n, inner - 1)),
            dma((3, n, inner - 1)),
            dma((n, inner - 1)),
            dma((n, inner - 1)),
            dma((n,)),
            dma((n,)),
            dma((2, planes)),
            dma((2, planes)),
            dma((2, planes - 1)),
            dma((2, planes - 1)),
        ],
        compiler_params=pltpu.CompilerParams(
            collective_id=0, has_side_effects=True, vmem_limit_bytes=61 * 1024 * 1024
        ),
        cost_estimate=pl.CostEstimate(
            flops=18 * n * count * width * hidden, bytes_accessed=20_000_000, transcendentals=0
        ),
    )(meta, tokens, tangents, cotangents, w_up[0], w_down[0], v_up[0])
    return (hvp_tokens, hvp_up[None], hvp_down[None])


def solution(mesh):
    in_specs = (P(("dp", "expert"), None),) * 5 + (P("expert", None, None),) * 3
    out_specs = (P(("dp", "expert"), None), P("expert", "dp", None), P("expert", None, "dp"))
    return jax.shard_map(
        per_device, mesh=mesh, in_specs=in_specs, out_specs=out_specs, check_vma=False
    )
```

```python
import functools
import math

import jax
import jax.numpy as jnp
from jax import lax
from jax.experimental import pallas as pl
from jax.experimental.pallas import tpu as pltpu
from jax.sharding import PartitionSpec as P

MESH = pl.DeviceIdType.MESH
F32 = jnp.float32
BF16 = jnp.bfloat16


def route_rows(routes, gates, expert_count):
    token_count = routes.shape[0]
    hit = routes[:, :, None] == jnp.arange(expert_count, dtype=jnp.int32)[None, None, :]
    mask = jnp.any(hit, axis=1)
    rank = jnp.cumsum(mask.astype(jnp.int32), axis=0) - 1
    slot = jnp.where(mask, rank, -1).astype(F32)
    gate = jnp.sum(jnp.where(hit, gates.astype(F32)[:, :, None], 0.0), axis=1)
    return jnp.concatenate([slot.T, gate.T], axis=0).reshape(2 * expert_count, token_count)


def layer_kernel(
    n, inner, cap, planes, scale,
    meta, tok, tan, cot, w_up, w_down, v_up,
    out, out_up, out_down,
    rows, hid, mbuf, gbuf, sbuf, hback, pbuf, wu, wd, vu,
    acc_up, acc_down, far_rows, far_hid,
    load_sem, own_send, fwd_send, g_recv, x_send, x_recv, h_send, h_recv, p_send, p_recv,
    row_send, row_recv, hid_send, hid_recv,
):
    me = lax.axis_index("expert")
    z = me // inner
    x = me % inner
    experts = n * inner
    tokens = gbuf.shape[2]
    rep = lax.axis_index("dp")
    y = rep // 2
    core = rep % 2
    part = acc_up.shape[0]
    replicas = 2 * planes
    sibling = y * 2 + 1 - core
    count = inner * cap

    def at(outer_pos, inner_pos):
        return {"expert": outer_pos * inner + inner_pos}

    def peer(o):
        return lax.rem(x + o, inner)

    def plane(o):
        return lax.rem(y + o, planes)

    own = [
        pltpu.make_async_copy(src, dst, load_sem.at[i])
        for i, (src, dst) in enumerate(
            [
                (meta, mbuf.at[z]),
                (tok, gbuf.at[0, z]),
                (tan, gbuf.at[1, z]),
                (cot, gbuf.at[2, z]),
                (w_up, wu),
                (v_up, vu),
                (w_down, wd),
            ]
        )
    ]
    for c in own:
        c.start()

    barrier = pltpu.get_barrier_semaphore()
    has_left = z > 0
    has_right = z < n - 1
    for cond, pos in ((has_left, z - 1), (has_right, z + 1)):

        @pl.when(cond)
        def _():
            pl.semaphore_signal(barrier, inc=1, device_id=at(pos, x), device_id_type=MESH)

    for o in range(1, inner):
        pl.semaphore_signal(barrier, inc=1, device_id=at(z, peer(o)), device_id_type=MESH)
    for o in range(1, n):
        far = lax.rem(z + o, n)

        @pl.when(jnp.logical_and(far != z - 1, far != z + 1))
        def _():
            pl.semaphore_signal(barrier, inc=1, device_id=at(far, x), device_id_type=MESH)

    for f in range(1, replicas):
        pl.semaphore_signal(
            barrier, inc=1, device_id={"dp": lax.rem(rep + f, replicas)}, device_id_type=MESH
        )

    pl.semaphore_wait(barrier, n - 1 + inner - 1 + replicas - 1)

    def block(a, j):
        return mbuf.at[j] if a == 0 else gbuf.at[a - 1, j]

    def hop(a, j, pos, send_sem):
        return pltpu.make_async_remote_copy(
            src_ref=block(a, j),
            dst_ref=block(a, j),
            send_sem=send_sem,
            recv_sem=g_recv.at[a, j],
            device_id=at(pos, x),
            device_id_type=MESH,
        )

    for a in range(4):
        own[a].wait()

        @pl.when(has_left)
        def _():
            hop(a, z, z - 1, own_send.at[a, 0]).start()

        @pl.when(has_right)
        def _():
            hop(a, z, z + 1, own_send.at[a, 1]).start()

    acc_up[...] = jnp.zeros_like(acc_up)
    acc_down[...] = jnp.zeros_like(acc_down)

    near = jnp.minimum(z, n - 1 - z)
    left_half = z < n - 1 - z

    def source(k):
        d = (k + 1) // 2
        toward = jnp.where(left_half, d, -d)
        close = jnp.where(k % 2 == 1, z + toward, z - toward)
        return jnp.where(k <= 2 * near, close, jnp.where(left_half, k, n - 1 - k))

    def picks(j):
        slots = lax.broadcasted_iota(jnp.int32, (cap, tokens), 0).astype(F32)
        ones, gated = [], []
        for o in range(inner):
            e = z * inner + peer(o)
            hit = mbuf[j, pl.ds(e, 1), :] == slots
            ones.append(jnp.where(hit, 1.0, 0.0))
            gated.append(jnp.where(hit, mbuf[j, pl.ds(experts + e, 1), :], 0.0))
        return jnp.concatenate(ones, axis=0), jnp.concatenate(gated, axis=0)

    def x_copy(a, j, o):
        return pltpu.make_async_remote_copy(
            src_ref=sbuf.at[j, a, o - 1],
            dst_ref=rows.at[j, a, pl.ds((inner - o) * cap, cap)],
            send_sem=x_send.at[a, j, o - 1],
            recv_sem=x_recv.at[a, j, inner - o - 1],
            device_id=at(z, peer(o)),
            device_id_type=MESH,
        )

    def x_arrival(a, j, o):
        return pltpu.make_async_remote_copy(
            src_ref=sbuf.at[j, a, o - 1],
            dst_ref=rows.at[j, a, pl.ds(o * cap, cap)],
            send_sem=x_send.at[a, j, o - 1],
            recv_sem=x_recv.at[a, j, o - 1],
            device_id=at(z, peer(o)),
            device_id_type=MESH,
        )

    def h_copy(j, o):
        return pltpu.make_async_remote_copy(
            src_ref=sbuf.at[j, 0, o - 1],
            dst_ref=hback.at[j, pl.ds((inner - o) * cap, cap)],
            send_sem=h_send.at[j, o - 1],
            recv_sem=h_recv.at[j, inner - o - 1],
            device_id=at(z, peer(o)),
            device_id_type=MESH,
        )

    def h_arrival(j, o):
        return pltpu.make_async_remote_copy(
            src_ref=sbuf.at[j, 0, o - 1],
            dst_ref=hback.at[j, pl.ds(o * cap, cap)],
            send_sem=h_send.at[j, o - 1],
            recv_sem=h_recv.at[j, o - 1],
            device_id=at(z, peer(o)),
            device_id_type=MESH,
        )

    def p_copy(j):
        return pltpu.make_async_remote_copy(
            src_ref=gbuf.at[0, j],
            dst_ref=pbuf.at[lax.rem(z - j + n, n) - 1],
            send_sem=p_send.at[j],
            recv_sem=p_recv.at[lax.rem(z - j + n, n) - 1],
            device_id=at(j, x),
            device_id_type=MESH,
        )

    def p_arrival(o):
        return pltpu.make_async_remote_copy(
            src_ref=gbuf.at[0, lax.rem(z + o, n)],
            dst_ref=pbuf.at[o - 1],
            send_sem=p_send.at[lax.rem(z + o, n)],
            recv_sem=p_recv.at[o - 1],
            device_id=at(lax.rem(z + o, n), x),
            device_id_type=MESH,
        )

    def take(a, j):
        forward_left = jnp.logical_and(j > z, has_left)
        forward_right = jnp.logical_and(j < z, has_right)

        @pl.when(j != z)
        def _():
            hop(a, j, z, fwd_send.at[a, j]).wait_recv()

            @pl.when(forward_left)
            def _():
                hop(a, j, z - 1, fwd_send.at[a, j]).start()

            @pl.when(forward_right)
            def _():
                hop(a, j, z + 1, fwd_send.at[a, j]).start()

    def pass_on(a, j, pick):
        got = jnp.dot(pick.astype(BF16), gbuf[a, j], preferred_element_type=F32).astype(BF16)
        for o in range(1, inner):
            sbuf[j, a, o - 1] = got[o * cap : (o + 1) * cap]
            x_copy(a, j, o).start()
        rows[j, a, pl.ds(0, cap)] = got[:cap]

    def nt(a, b):
        return lax.dot_general(a, b, (((1,), (1,)), ((), ())), preferred_element_type=F32)

    def tn(a, b):
        return lax.dot_general(a, b, (((0,), (0,)), ((), ())), preferred_element_type=F32)

    def columns(r):
        return pl.ds(pl.multiple_of(r * part, part), part)

    def place(there, sender):
        return lax.rem(sender - there + replicas, replicas) - 1

    def row_copy(a, j, f):
        r = lax.rem(rep + f, replicas)
        return pltpu.make_async_remote_copy(
            src_ref=rows.at[j, a, :, columns(r)],
            dst_ref=far_rows.at[j, a, replicas - f - 1],
            send_sem=row_send.at[a, j, f - 1],
            recv_sem=row_recv.at[a, j, replicas - f - 1],
            device_id={"dp": r},
            device_id_type=MESH,
        )

    def row_arrival(a, j, f):
        return pltpu.make_async_remote_copy(
            src_ref=rows.at[j, a, :, columns(rep)],
            dst_ref=far_rows.at[j, a, f - 1],
            send_sem=row_send.at[a, j, f - 1],
            recv_sem=row_recv.at[a, j, f - 1],
            device_id={"dp": lax.rem(rep + f, replicas)},
            device_id_type=MESH,
        )

    def hid_copy(h, j, o):
        r = sibling if o == 0 else plane(o) * 2 + core
        return pltpu.make_async_remote_copy(
            src_ref=hid.at[j, h],
            dst_ref=far_hid.at[j, h, place(r, rep)],
            send_sem=hid_send.at[h, j, place(rep, r)],
            recv_sem=hid_recv.at[h, j, place(r, rep)],
            device_id={"dp": r},
            device_id_type=MESH,
        )

    def hid_relay(h, j, o):
        d = plane(o) * 2 + core
        return pltpu.make_async_remote_copy(
            src_ref=far_hid.at[j, h, place(rep, d)],
            dst_ref=far_hid.at[j, h, place(sibling, d)],
            send_sem=hid_send.at[h, j, place(rep, plane(o) * 2 + 1 - core)],
            recv_sem=hid_recv.at[h, j, place(sibling, d)],
            device_id={"dp": sibling},
            device_id_type=MESH,
        )

    def hid_arrival(h, j, d):
        return pltpu.make_async_remote_copy(
            src_ref=hid.at[j, h],
            dst_ref=far_hid.at[j, h, place(rep, d)],
            send_sem=hid_send.at[h, j, place(rep, d)],
            recv_sem=hid_recv.at[h, j, place(rep, d)],
            device_id={"dp": d},
            device_id_type=MESH,
        )

    def relay(h, j):
        for o in range(1, planes):
            hid_arrival(h, j, plane(o) * 2 + core).wait_recv()
            hid_relay(h, j, o).start()

    def absorb(j):
        depth = (replicas - 1) * count
        acc_down[...] += tn(hid[j, 2], rows[j, 2, :, columns(rep)])
        acc_up[...] += tn(
            rows[j, pl.ds(0, 2), :, columns(rep)].reshape(2 * count, part),
            hid[j, pl.ds(0, 2)].reshape(2 * count, hid.shape[3]),
        )

        def arrived(i):
            for f in range(1, replicas):
                row_arrival(i, j, f).wait_recv()
            for o in range(planes):
                hid_arrival(i, j, sibling if o == 0 else plane(o) * 2 + 1 - core).wait_recv()

        arrived(2)
        acc_down[...] += tn(
            far_hid[j, 2].reshape(depth, hid.shape[3]), far_rows[j, 2].reshape(depth, part)
        )
        arrived(1)
        arrived(0)
        acc_up[...] += tn(
            far_rows[j, pl.ds(0, 2)].reshape(2 * depth, part),
            far_hid[j, pl.ds(0, 2)].reshape(2 * depth, hid.shape[3]),
        )

    def landed(a, j):
        for o in range(1, inner):
            x_arrival(a, j, o).wait_recv()
        for f in range(1, replicas):
            row_copy(a, j, f).start()

    def send_hidden(h, j, value):
        hid[j, h] = value.astype(BF16)
        for o in range(1, planes):
            hid_copy(h, j, o).start()
        hid_copy(h, j, 0).start()

    def first_part(k):
        j = source(k)
        take(0, j)
        ones, _ = picks(j)
        for a in range(2):
            take(a + 1, j)
            pass_on(a, j, ones)

    def second_part(k):
        j = source(k)

        @pl.when(k == 0)
        def _():
            own[4].wait()
            own[5].wait()

        landed(0, j)
        landed(1, j)
        both = rows[j, pl.ds(0, 2)].reshape(2 * count, rows.shape[3])
        up = jnp.dot(both, wu[...], preferred_element_type=F32)
        act = up[:count]
        act_tan = up[count:] + jnp.dot(rows[j, 0], vu[...], preferred_element_type=F32)
        s = 1.0 / (1.0 + jnp.exp(-act))
        s1 = s * (1.0 + act * (1.0 - s))
        s2 = s * (1.0 - s) * (2.0 + act * (1.0 - 2.0 * s))
        s2_tan = s2 * act_tan
        send_hidden(2, j, s1 * act_tan)

        take(3, j)
        _, gated = picks(j)
        pass_on(2, j, gated)

        @pl.when(k == 0)
        def _():
            own[6].wait()

        landed(2, j)
        back = nt(rows[j, 2], wd[...])
        send_hidden(1, j, back * s1)
        send_hidden(0, j, back * s2_tan)
        ha = (nt(hid[j, 0], wu[...]) + nt(hid[j, 1], vu[...])).astype(BF16)
        for o in range(1, inner):
            x_copy(0, j, o).wait_send()
            sbuf[j, 0, o - 1] = ha[o * cap : (o + 1) * cap]
            h_copy(j, o).start()
        hback[j, pl.ds(0, cap)] = ha[:cap]

    def sent(a, j):
        @pl.when(jnp.logical_and(j == z, has_left))
        def _():
            hop(a, z, z, own_send.at[a, 0]).wait_send()

        @pl.when(jnp.logical_and(j == z, has_right))
        def _():
            hop(a, z, z, own_send.at[a, 1]).wait_send()

        forwarded = jnp.logical_or(
            jnp.logical_and(j > z, has_left), jnp.logical_and(j < z, has_right)
        )

        @pl.when(forwarded)
        def _():
            hop(a, j, z, fwd_send.at[a, j]).wait_send()

    def give(j):
        for o in range(1, inner):
            h_arrival(j, o).wait_recv()
        ones, _ = picks(j)
        part = jnp.dot(ones.T.astype(BF16), hback[j], preferred_element_type=F32).astype(BF16)

        sent(1, j)
        gbuf[0, j] = part

        @pl.when(j != z)
        def _():
            p_copy(j).start()

    def step(k, carry):
        @pl.when(k < n)
        def _():
            first_part(k)

        @pl.when(k >= 1)
        def _():
            j = source(k - 1)
            relay(2, j)
            give(j)
            relay(1, j)
            relay(0, j)
            absorb(j)

        @pl.when(k < n)
        def _():
            second_part(k)

        return carry

    lax.fori_loop(0, n + 1, step, 0)

    out_up[...] = (acc_up[...] * scale).astype(BF16)
    out_down[...] = (acc_down[...] * scale).astype(BF16)

    total = gbuf[0, z].astype(F32)
    for o in range(1, n):
        p_arrival(o).wait_recv()
        total = total + pbuf[o - 1].astype(F32)
    out[...] = total.astype(BF16)

    def drain(j, carry):
        for a in (0, 2, 3):
            sent(a, j)

        for o in range(1, inner):
            for a in range(1, 3):
                x_copy(a, j, o).wait_send()
            h_copy(j, o).wait_send()

        @pl.when(j != z)
        def _():
            p_copy(j).wait_send()

        for a in range(3):
            for f in range(1, replicas):
                row_copy(a, j, f).wait_send()
            for o in range(planes):
                hid_copy(a, j, o).wait_send()
            for o in range(1, planes):
                hid_relay(a, j, o).wait_send()

        return carry

    lax.fori_loop(0, n, drain, 0)


def per_device(tokens, tangents, cotangents, routes, gates, w_up, w_down, v_up):
    token_count, width = tokens.shape
    route_count = routes.shape[1]
    experts = lax.axis_size("expert")
    replicas = lax.axis_size("dp")
    hidden = w_up.shape[2]
    cap = max(2, token_count * route_count * 2 // experts)
    scale = 1.0 / math.sqrt(token_count * route_count * replicas)
    n = 4
    inner = experts // n
    meta = route_rows(routes, gates, experts)
    count = inner * cap
    planes = replicas // 2
    part = width // replicas
    vmem = pl.BlockSpec(memory_space=pltpu.VMEM)
    hbm = pl.BlockSpec(memory_space=pl.ANY)
    dma = pltpu.SemaphoreType.DMA
    up, down = (part, hidden), (hidden, part)
    hvp_tokens, hvp_up, hvp_down = pl.pallas_call(
        functools.partial(layer_kernel, n, inner, cap, planes, scale),
        out_shape=(
            jax.ShapeDtypeStruct((token_count, width), BF16),
            jax.ShapeDtypeStruct(up, BF16),
            jax.ShapeDtypeStruct(down, BF16),
        ),
        in_specs=[hbm] * 7,
        out_specs=(vmem, vmem, vmem),
        scratch_shapes=[
            pltpu.VMEM((n, 3, count, width), BF16),
            pltpu.VMEM((n, 3, count, hidden), BF16),
            pltpu.VMEM((n, 2 * experts, token_count), F32),
            pltpu.VMEM((3, n, token_count, width), BF16),
            pltpu.VMEM((n, 3, inner - 1, cap, width), BF16),
            pltpu.VMEM((n, count, width), BF16),
            pltpu.VMEM((n - 1, token_count, width), BF16),
            pltpu.VMEM((width, hidden), BF16),
            pltpu.VMEM((hidden, width), BF16),
            pltpu.VMEM((width, hidden), BF16),
            pltpu.VMEM(up, F32),
            pltpu.VMEM(down, F32),
            pltpu.VMEM((n, 3, replicas - 1, count, part), BF16),
            pltpu.VMEM((n, 3, replicas - 1, count, hidden), BF16),
            dma((7,)),
            dma((4, 2)),
            dma((4, n)),
            dma((4, n)),
            dma((3, n, inner - 1)),
            dma((3, n, inner - 1)),
            dma((n, inner - 1)),
            dma((n, inner - 1)),
            dma((n,)),
            dma((n,)),
            dma((3, n, replicas - 1)),
            dma((3, n, replicas - 1)),
            dma((3, n, replicas - 1)),
            dma((3, n, replicas - 1)),
        ],
        compiler_params=pltpu.CompilerParams(
            collective_id=0, has_side_effects=True, vmem_limit_bytes=61 * 1024 * 1024
        ),
        cost_estimate=pl.CostEstimate(
            flops=18 * n * count * width * hidden, bytes_accessed=20_000_000, transcendentals=0
        ),
    )(meta, tokens, tangents, cotangents, w_up[0], w_down[0], v_up[0])
    return (hvp_tokens, hvp_up[None], hvp_down[None])


def solution(mesh):
    in_specs = (P(("dp", "expert"), None),) * 5 + (P("expert", None, None),) * 3
    out_specs = (P(("dp", "expert"), None), P("expert", "dp", None), P("expert", None, "dp"))
    return jax.shard_map(
        per_device, mesh=mesh, in_specs=in_specs, out_specs=out_specs, check_vma=False
    )
```

```python
import functools
import math

import jax
import jax.numpy as jnp
from jax import lax
from jax.experimental import pallas as pl
from jax.experimental.pallas import tpu as pltpu
from jax.sharding import PartitionSpec as P

MESH = pl.DeviceIdType.MESH
F32 = jnp.float32
BF16 = jnp.bfloat16


def route_rows(routes, gates, expert_count):
    token_count = routes.shape[0]
    hit = routes[:, :, None] == jnp.arange(expert_count, dtype=jnp.int32)[None, None, :]
    mask = jnp.any(hit, axis=1)
    rank = jnp.cumsum(mask.astype(jnp.int32), axis=0) - 1
    slot = jnp.where(mask, rank, -1).astype(F32)
    gate = jnp.sum(jnp.where(hit, gates.astype(F32)[:, :, None], 0.0), axis=1)
    return jnp.concatenate([slot.T, gate.T], axis=0).reshape(2 * expert_count, token_count)


def layer_kernel(
    n, inner, cap, planes, scale,
    meta, tok, tan, cot, w_up, w_down, v_up,
    out, out_up, out_down,
    rows, hid, mbuf, gbuf, sbuf, hback, pbuf, wu, wd, vu,
    acc_up, acc_down, core_out_up, core_out_down, core_in_up, core_in_down,
    plane_out_up, plane_out_down, plane_in_up, plane_in_down,
    load_sem, own_send, fwd_send, g_recv, x_send, x_recv, h_send, h_recv, p_send, p_recv,
    core_send, core_recv, plane_send, plane_recv,
):
    me = lax.axis_index("expert")
    z = me // inner
    x = me % inner
    experts = n * inner
    tokens = gbuf.shape[2]
    rep = lax.axis_index("dp")
    y = rep // 2
    core = rep % 2
    part = acc_up.shape[1]
    count = inner * cap

    def at(outer_pos, inner_pos):
        return {"expert": outer_pos * inner + inner_pos}

    def peer(o):
        return lax.rem(x + o, inner)

    def plane(o):
        return lax.rem(y + o, planes)

    own = [
        pltpu.make_async_copy(src, dst, load_sem.at[i])
        for i, (src, dst) in enumerate(
            [
                (meta, mbuf.at[z]),
                (tok, gbuf.at[0, z]),
                (tan, gbuf.at[1, z]),
                (cot, gbuf.at[2, z]),
                (w_up, wu),
                (v_up, vu),
                (w_down, wd),
            ]
        )
    ]
    for c in own:
        c.start()

    barrier = pltpu.get_barrier_semaphore()
    has_left = z > 0
    has_right = z < n - 1
    for cond, pos in ((has_left, z - 1), (has_right, z + 1)):

        @pl.when(cond)
        def _():
            pl.semaphore_signal(barrier, inc=1, device_id=at(pos, x), device_id_type=MESH)

    for o in range(1, inner):
        pl.semaphore_signal(barrier, inc=1, device_id=at(z, peer(o)), device_id_type=MESH)
    for o in range(1, n):
        far = lax.rem(z + o, n)

        @pl.when(jnp.logical_and(far != z - 1, far != z + 1))
        def _():
            pl.semaphore_signal(barrier, inc=1, device_id=at(far, x), device_id_type=MESH)

    pl.semaphore_signal(
        barrier, inc=1, device_id={"dp": y * 2 + 1 - core}, device_id_type=MESH
    )
    for o in range(1, planes):
        pl.semaphore_signal(
            barrier, inc=1, device_id={"dp": plane(o) * 2 + core}, device_id_type=MESH
        )

    pl.semaphore_wait(barrier, n - 1 + inner - 1 + planes)

    def block(a, j):
        return mbuf.at[j] if a == 0 else gbuf.at[a - 1, j]

    def hop(a, j, pos, send_sem):
        return pltpu.make_async_remote_copy(
            src_ref=block(a, j),
            dst_ref=block(a, j),
            send_sem=send_sem,
            recv_sem=g_recv.at[a, j],
            device_id=at(pos, x),
            device_id_type=MESH,
        )

    for a in range(4):
        own[a].wait()

        @pl.when(has_left)
        def _():
            hop(a, z, z - 1, own_send.at[a, 0]).start()

        @pl.when(has_right)
        def _():
            hop(a, z, z + 1, own_send.at[a, 1]).start()

    acc_up[...] = jnp.zeros_like(acc_up)
    acc_down[...] = jnp.zeros_like(acc_down)

    near = jnp.minimum(z, n - 1 - z)
    left_half = z < n - 1 - z

    def source(k):
        d = (k + 1) // 2
        toward = jnp.where(left_half, d, -d)
        close = jnp.where(k % 2 == 1, z + toward, z - toward)
        return jnp.where(k <= 2 * near, close, jnp.where(left_half, k, n - 1 - k))

    def picks(j):
        slots = lax.broadcasted_iota(jnp.int32, (cap, tokens), 0).astype(F32)
        ones, gated = [], []
        for o in range(inner):
            e = z * inner + peer(o)
            hit = mbuf[j, pl.ds(e, 1), :] == slots
            ones.append(jnp.where(hit, 1.0, 0.0))
            gated.append(jnp.where(hit, mbuf[j, pl.ds(experts + e, 1), :], 0.0))
        return jnp.concatenate(ones, axis=0), jnp.concatenate(gated, axis=0)

    def x_copy(a, j, o):
        return pltpu.make_async_remote_copy(
            src_ref=sbuf.at[j, a, o - 1],
            dst_ref=rows.at[j, a, pl.ds((inner - o) * cap, cap)],
            send_sem=x_send.at[a, j, o - 1],
            recv_sem=x_recv.at[a, j, inner - o - 1],
            device_id=at(z, peer(o)),
            device_id_type=MESH,
        )

    def x_arrival(a, j, o):
        return pltpu.make_async_remote_copy(
            src_ref=sbuf.at[j, a, o - 1],
            dst_ref=rows.at[j, a, pl.ds(o * cap, cap)],
            send_sem=x_send.at[a, j, o - 1],
            recv_sem=x_recv.at[a, j, o - 1],
            device_id=at(z, peer(o)),
            device_id_type=MESH,
        )

    def h_copy(j, o):
        return pltpu.make_async_remote_copy(
            src_ref=sbuf.at[j, 0, o - 1],
            dst_ref=hback.at[j, pl.ds((inner - o) * cap, cap)],
            send_sem=h_send.at[j, o - 1],
            recv_sem=h_recv.at[j, inner - o - 1],
            device_id=at(z, peer(o)),
            device_id_type=MESH,
        )

    def h_arrival(j, o):
        return pltpu.make_async_remote_copy(
            src_ref=sbuf.at[j, 0, o - 1],
            dst_ref=hback.at[j, pl.ds(o * cap, cap)],
            send_sem=h_send.at[j, o - 1],
            recv_sem=h_recv.at[j, o - 1],
            device_id=at(z, peer(o)),
            device_id_type=MESH,
        )

    def p_copy(j):
        return pltpu.make_async_remote_copy(
            src_ref=gbuf.at[0, j],
            dst_ref=pbuf.at[lax.rem(z - j + n, n) - 1],
            send_sem=p_send.at[j],
            recv_sem=p_recv.at[lax.rem(z - j + n, n) - 1],
            device_id=at(j, x),
            device_id_type=MESH,
        )

    def p_arrival(o):
        return pltpu.make_async_remote_copy(
            src_ref=gbuf.at[0, lax.rem(z + o, n)],
            dst_ref=pbuf.at[o - 1],
            send_sem=p_send.at[lax.rem(z + o, n)],
            recv_sem=p_recv.at[o - 1],
            device_id=at(lax.rem(z + o, n), x),
            device_id_type=MESH,
        )

    def take(a, j):
        forward_left = jnp.logical_and(j > z, has_left)
        forward_right = jnp.logical_and(j < z, has_right)

        @pl.when(j != z)
        def _():
            hop(a, j, z, fwd_send.at[a, j]).wait_recv()

            @pl.when(forward_left)
            def _():
                hop(a, j, z - 1, fwd_send.at[a, j]).start()

            @pl.when(forward_right)
            def _():
                hop(a, j, z + 1, fwd_send.at[a, j]).start()

    def paired(k):
        return jnp.logical_and(k % 2 == 1, k < 2 * near)

    def pass_on(a, j, pick):
        got = jnp.dot(pick.astype(BF16), gbuf[a, j], preferred_element_type=F32).astype(BF16)
        for o in range(1, inner):
            sbuf[j, a, o - 1] = got[o * cap : (o + 1) * cap]
            x_copy(a, j, o).start()
        rows[j, a, pl.ds(0, cap)] = got[:cap]

    def nt(a, b):
        return lax.dot_general(a, b, (((1,), (1,)), ((), ())), preferred_element_type=F32)

    def tn(a, b):
        return lax.dot_general(a, b, (((0,), (0,)), ((), ())), preferred_element_type=F32)

    def part_up(j, c):
        columns = pl.ds(pl.multiple_of(c * part, part), part)
        left = rows[j, pl.ds(0, 2), :, columns].reshape(2 * inner * cap, part)
        return tn(left, hid[j, pl.ds(0, 2)].reshape(2 * inner * cap, hid.shape[3]))

    def part_down(j, c):
        columns = pl.ds(pl.multiple_of(c * part, part), part)
        return tn(hid[j, 2], rows[j, 2, :, columns])

    def gather_part(j, c, carry):
        acc_up[c] += part_up(j, c)
        acc_down[c] += part_down(j, c)
        return carry

    core_out, core_in = (core_out_up, core_out_down), (core_in_up, core_in_down)
    plane_out, plane_in = (plane_out_up, plane_out_down), (plane_in_up, plane_in_down)
    accs, parts = (acc_up, acc_down), (part_up, part_down)

    def core_copy(half, yy):
        return pltpu.make_async_remote_copy(
            src_ref=core_out[half].at[yy],
            dst_ref=core_in[half].at[yy],
            send_sem=core_send.at[half, yy],
            recv_sem=core_recv.at[half, yy],
            device_id={"dp": y * 2 + 1 - core},
            device_id_type=MESH,
        )

    def plane_copy(half, o):
        return pltpu.make_async_remote_copy(
            src_ref=plane_out[half].at[o - 1],
            dst_ref=plane_in[half].at[planes - o - 1],
            send_sem=plane_send.at[half, o - 1],
            recv_sem=plane_recv.at[half, planes - o - 1],
            device_id={"dp": plane(o) * 2 + core},
            device_id_type=MESH,
        )

    def plane_arrival(half, o):
        return pltpu.make_async_remote_copy(
            src_ref=plane_out[half].at[o - 1],
            dst_ref=plane_in[half].at[o - 1],
            send_sem=plane_send.at[half, o - 1],
            recv_sem=plane_recv.at[half, o - 1],
            device_id={"dp": plane(o) * 2 + core},
            device_id_type=MESH,
        )

    def share(j):
        for o in range(1, planes + 1):
            yy = plane(o)
            for half in range(2):
                c = yy * 2 + 1 - core
                mine = accs[half][c] + parts[half](j, c)
                core_out[half][yy] = (mine * scale).astype(BF16)
                core_copy(half, yy).start()
            for half in range(2):
                c = yy * 2 + core
                mine = (accs[half][c] + parts[half](j, c)) * scale
                if o < planes:
                    core_copy(half, yy).wait_recv()
                    mine = mine + core_in[half][yy].astype(F32)
                    plane_out[half][o - 1] = mine.astype(BF16)
                    plane_copy(half, o).start()
                else:
                    accs[half][c] = mine

    def landed(a, j):
        for o in range(1, inner):
            x_arrival(a, j, o).wait_recv()

    inside = jnp.logical_and(has_left, has_right)

    def pass_cotangents(j):
        _, gated = picks(j)
        pass_on(2, j, gated)

    def first_part(k):
        j = source(k)
        early = jnp.logical_and(k > 0, paired(k - 1))

        @pl.when(jnp.logical_not(early))
        def _():
            take(0, j)

        ones, _ = picks(j)
        for a in range(2):

            @pl.when(jnp.logical_not(early))
            def _():
                take(a + 1, j)

            pass_on(a, j, ones)

        @pl.when(inside)
        def _():
            @pl.when(jnp.logical_not(early))
            def _():
                take(3, j)

            pass_cotangents(j)

            @pl.when(paired(k))
            def _():
                for a in range(4):
                    take(a, source(k + 1))

    def second_part(k):
        j = source(k)

        @pl.when(k == 0)
        def _():
            own[4].wait()
            own[5].wait()

        landed(0, j)
        landed(1, j)
        both = rows[j, pl.ds(0, 2)].reshape(2 * count, rows.shape[3])
        up = jnp.dot(both, wu[...], preferred_element_type=F32)
        act = up[:count]
        act_tan = up[count:] + jnp.dot(rows[j, 0], vu[...], preferred_element_type=F32)
        s = 1.0 / (1.0 + jnp.exp(-act))
        s1 = s * (1.0 + act * (1.0 - s))
        s2 = s * (1.0 - s) * (2.0 + act * (1.0 - 2.0 * s))
        s2_tan = s2 * act_tan
        hid[j, 2] = (s1 * act_tan).astype(BF16)

        @pl.when(jnp.logical_not(inside))
        def _():
            take(3, j)
            pass_cotangents(j)

        @pl.when(k == 0)
        def _():
            own[6].wait()

        landed(2, j)
        back = nt(rows[j, 2], wd[...])
        hid[j, 1] = (back * s1).astype(BF16)
        hid[j, 0] = (back * s2_tan).astype(BF16)

        @pl.when(k == n - 1)
        def _():
            share(j)

        ha = (nt(hid[j, 0], wu[...]) + nt(hid[j, 1], vu[...])).astype(BF16)
        for o in range(1, inner):
            x_copy(0, j, o).wait_send()
            sbuf[j, 0, o - 1] = ha[o * cap : (o + 1) * cap]
            h_copy(j, o).start()
        hback[j, pl.ds(0, cap)] = ha[:cap]

    def sent(a, j):
        @pl.when(jnp.logical_and(j == z, has_left))
        def _():
            hop(a, z, z, own_send.at[a, 0]).wait_send()

        @pl.when(jnp.logical_and(j == z, has_right))
        def _():
            hop(a, z, z, own_send.at[a, 1]).wait_send()

        forwarded = jnp.logical_or(
            jnp.logical_and(j > z, has_left), jnp.logical_and(j < z, has_right)
        )

        @pl.when(forwarded)
        def _():
            hop(a, j, z, fwd_send.at[a, j]).wait_send()

    def give(j):
        for o in range(1, inner):
            h_arrival(j, o).wait_recv()
        ones, _ = picks(j)
        part = jnp.dot(ones.T.astype(BF16), hback[j], preferred_element_type=F32).astype(BF16)

        sent(1, j)
        gbuf[0, j] = part

        @pl.when(j != z)
        def _():
            p_copy(j).start()

    def step(k, carry):
        @pl.when(k < n)
        def _():
            first_part(k)

        at_work = jnp.where(inside, k - 1, k)

        @pl.when(jnp.logical_and(at_work >= 1, at_work <= n))
        def _():
            j = source(at_work - 1)
            give(j)

            @pl.when(at_work < n)
            def _():
                lax.fori_loop(0, 2 * planes, functools.partial(gather_part, j), 0)

        @pl.when(jnp.logical_and(at_work >= 0, at_work < n))
        def _():
            second_part(at_work)

        return carry

    lax.fori_loop(0, n + 2, step, 0)

    total = gbuf[0, z].astype(F32)
    for o in range(1, n):
        p_arrival(o).wait_recv()
        total = total + pbuf[o - 1].astype(F32)
    out[...] = total.astype(BF16)

    for half, result in enumerate((out_up, out_down)):
        core_copy(half, y).wait_recv()
        total = accs[half][y * 2 + core] + core_in[half][y].astype(F32)
        for o in range(1, planes):
            plane_arrival(half, o).wait_recv()
            total = total + plane_in[half][o - 1].astype(F32)
        result[...] = total.astype(BF16)
        for o in range(1, planes):
            plane_copy(half, o).wait_send()
        for yy in range(planes):
            core_copy(half, yy).wait_send()

    for j in range(n):
        for a in (0, 2, 3):
            sent(a, j)

        for o in range(1, inner):
            for a in range(1, 3):
                x_copy(a, j, o).wait_send()
            h_copy(j, o).wait_send()

        @pl.when(j != z)
        def _():
            p_copy(j).wait_send()


def per_device(tokens, tangents, cotangents, routes, gates, w_up, w_down, v_up):
    token_count, width = tokens.shape
    route_count = routes.shape[1]
    experts = lax.axis_size("expert")
    replicas = lax.axis_size("dp")
    hidden = w_up.shape[2]
    cap = max(2, token_count * route_count * 2 // experts)
    scale = 1.0 / math.sqrt(token_count * route_count * replicas)
    n = 4
    inner = experts // n
    meta = route_rows(routes, gates, experts)
    count = inner * cap
    planes = replicas // 2
    part = width // replicas
    vmem = pl.BlockSpec(memory_space=pltpu.VMEM)
    hbm = pl.BlockSpec(memory_space=pl.ANY)
    dma = pltpu.SemaphoreType.DMA
    up, down = (part, hidden), (hidden, part)
    hvp_tokens, hvp_up, hvp_down = pl.pallas_call(
        functools.partial(layer_kernel, n, inner, cap, planes, scale),
        out_shape=(
            jax.ShapeDtypeStruct((token_count, width), BF16),
            jax.ShapeDtypeStruct(up, BF16),
            jax.ShapeDtypeStruct(down, BF16),
        ),
        in_specs=[hbm] * 7,
        out_specs=(vmem, vmem, vmem),
        scratch_shapes=[
            pltpu.VMEM((n, 3, count, width), BF16),
            pltpu.VMEM((n, 3, count, hidden), BF16),
            pltpu.VMEM((n, 2 * experts, token_count), F32),
            pltpu.VMEM((3, n, token_count, width), BF16),
            pltpu.VMEM((n, 3, inner - 1, cap, width), BF16),
            pltpu.VMEM((n, count, width), BF16),
            pltpu.VMEM((n - 1, token_count, width), BF16),
            pltpu.VMEM((width, hidden), BF16),
            pltpu.VMEM((hidden, width), BF16),
            pltpu.VMEM((width, hidden), BF16),
            pltpu.VMEM((replicas,) + up, F32),
            pltpu.VMEM((replicas,) + down, F32),
            pltpu.VMEM((planes,) + up, BF16),
            pltpu.VMEM((planes,) + down, BF16),
            pltpu.VMEM((planes,) + up, BF16),
            pltpu.VMEM((planes,) + down, BF16),
            pltpu.VMEM((planes - 1,) + up, BF16),
            pltpu.VMEM((planes - 1,) + down, BF16),
            pltpu.VMEM((planes - 1,) + up, BF16),
            pltpu.VMEM((planes - 1,) + down, BF16),
            dma((7,)),
            dma((4, 2)),
            dma((4, n)),
            dma((4, n)),
            dma((3, n, inner - 1)),
            dma((3, n, inner - 1)),
            dma((n, inner - 1)),
            dma((n, inner - 1)),
            dma((n,)),
            dma((n,)),
            dma((2, planes)),
            dma((2, planes)),
            dma((2, planes - 1)),
            dma((2, planes - 1)),
        ],
        compiler_params=pltpu.CompilerParams(
            collective_id=0, has_side_effects=True, vmem_limit_bytes=61 * 1024 * 1024
        ),
        cost_estimate=pl.CostEstimate(
            flops=18 * n * count * width * hidden, bytes_accessed=20_000_000, transcendentals=0
        ),
    )(meta, tokens, tangents, cotangents, w_up[0], w_down[0], v_up[0])
    return (hvp_tokens, hvp_up[None], hvp_down[None])


def solution(mesh):
    in_specs = (P(("dp", "expert"), None),) * 5 + (P("expert", None, None),) * 3
    out_specs = (P(("dp", "expert"), None), P("expert", "dp", None), P("expert", None, "dp"))
    return jax.shard_map(
        per_device, mesh=mesh, in_specs=in_specs, out_specs=out_specs, check_vma=False
    )
```
